512 devices in a mesh: row: 16 (over x, z_hi), col: 32 (over y, z_lo, core).
Axes of the slice: x: 4, y: 8, z: 8 (z_hi: 4, z_lo: 2; z = z_hi * 2 + z_lo), core: 2. Of those that a mesh axis runs over, the one named last changes fastest.
Arguments:
- features: bfloat16 [32768, 256], P(('col', 'row')), may hold values from -6 to 6
- cotangent: bfloat16 [32768, 256], P(('col', 'row')), may hold values from -0.09375 to 0.09375
- w_first: bfloat16 [256, 256], replicated, may hold values from -0.375 to 0.375
- w_second: bfloat16 [256, 256], replicated, may hold values from -0.375 to 0.375
- adjacency_tiles: bfloat16 [16, 32, 64, 128, 128], P('row', 'col'), may hold values from -0.046875 to 0.046875
- tile_ids: int32 [16, 32, 2, 64], P('row', 'col'), may hold values from 0 to 7, as said below
- counts: int32 [16, 32], P('row', 'col'), may hold values from 16 to 64, as said below
Outputs:
- item_out: bfloat16 [32768, 256], P(('col', 'row'))
- grad_w1: float32 [256, 256], replicated
- grad_w2: float32 [256, 256], replicated
The draws below stay inside these ranges and needn't reach their ends.
Inputs may be any that keep to these rules, and one draw needn't show every extreme that they name: `tile_ids`: in every block each of the 64 tile positions occurs exactly once over the 64 slots. A block holds either 64 live slots or at most 32; blocks with 64 live slots have r < 8 and c < 16; only the first counts[r, c] slots of a block are live.
All inputs are finite; a program needn't handle non-finite values.
Results may differ from the reference program's by a relative error of at most 0.018.
Values may be sent and summed in bfloat16 or wider, within the bound.
No kernel may reach another device: no remote copies, remote signals or barrier semaphores. Data moves between devices by JAX's collectives and lax.ppermute only.
A program may use at most 64 MiB of HBM per device.

```python
import jax
import jax.numpy as jnp
from jax import lax

WIDTH = 256
TILE = 128
ROW_TILES = 8
COL_TILES = 8
SLOTS = 64
ITEMS = 32768
N_ROW = 16
N_COL = 32


def draw_tile_ids(key, part):
    key = jax.random.fold_in(key, 11)
    keys = jax.random.split(key, N_ROW * N_COL)
    positions = ROW_TILES * COL_TILES
    orders = jax.vmap(lambda single: jax.random.permutation(single, positions))(keys)
    orders = orders.reshape(N_ROW, N_COL, positions).astype(jnp.int32)
    return jnp.stack([orders // COL_TILES, orders % COL_TILES], axis=2).astype(jnp.int32)


def draw_counts(key, part):
    key = jax.random.fold_in(key, 23)
    key_light, key_busy, key_pick = jax.random.split(key, 3)
    lowest = max(SLOTS // 4, 1)
    light = jax.random.randint(key_light, (N_ROW, N_COL), lowest, SLOTS // 2 + 1)
    row_pos = jnp.arange(N_ROW, dtype=jnp.int32)[:, None]
    col_pos = jnp.arange(N_COL, dtype=jnp.int32)[None, :]
    quadrant = (row_pos < N_ROW // 2) & (col_pos < N_COL // 2)
    busy = (jax.random.randint(key_busy, (N_ROW, N_COL), 0, 2) == 0) & quadrant
    filled = jnp.where(busy, SLOTS, light).astype(jnp.int32)
    picks = jax.random.randint(key_pick, (4,), 0, 4096)
    busy_row = picks[0] % (N_ROW // 2)
    busy_col = picks[1] % (N_COL // 2)
    low_row = N_ROW // 2 + picks[2] % (N_ROW // 2)
    low_col = picks[3] % N_COL
    filled = filled.at[busy_row, busy_col].set(SLOTS).at[low_row, low_col].set(lowest)
    return filled.astype(jnp.int32)


def steps_of(stream_key, shape, cuts, least, top_value):
    level = 1.0
    for dim, shards_of in cuts:
        steps = jax.random.uniform(jax.random.fold_in(jax.random.fold_in(stream_key, 6), dim), (shards_of,), jnp.float32, least / len(cuts), top_value / len(cuts))
        level = level * jnp.repeat(jnp.exp(steps), shape[dim] // shards_of).reshape((-1,) + (1,) * (len(shape) - 1 - dim))
    return level


def gaussian(own_key, shape, width, most, pieces=(), held_as=jnp.bfloat16):
    loudness = steps_of(own_key, shape, pieces, -0.22, 0.18) if pieces else 1.0
    array = jax.random.normal(own_key, shape, jnp.float32) * width * loudness
    return jnp.minimum(jnp.maximum(array, -most), most).astype(held_as)


def setup_inputs(seed: int = 0) -> dict:
    seeds = jax.random.split(jax.random.key(seed), 8)
    features = gaussian(seeds[0], (ITEMS, WIDTH), 1.0, 6.0, ((0, 512),))
    cotangent = gaussian(seeds[1], (ITEMS, WIDTH), (2.0 / (TILE * ROW_TILES * N_ROW) ** 0.5), 0.09375, ((0, 512),))
    w_first = gaussian(seeds[2], (WIDTH, WIDTH), WIDTH ** -0.5, 0.375)
    w_second = gaussian(seeds[3], (WIDTH, WIDTH), WIDTH ** -0.5, 0.375)
    adjacency_tiles = gaussian(seeds[4], (N_ROW, N_COL, SLOTS, TILE, TILE), (TILE * COL_TILES * N_COL // 2) ** -0.5, 0.046875, ((0, 16), (1, 32)))
    tile_ids = draw_tile_ids(jax.random.fold_in(seeds[7], 71), 0)
    counts = draw_counts(jax.random.fold_in(seeds[7], 71), 0)
    return dict(features=features, cotangent=cotangent, w_first=w_first, w_second=w_second, adjacency_tiles=adjacency_tiles, tile_ids=tile_ids, counts=counts)


def spread_users(adjacency_tiles, tile_ids, counts, items):
    feat_width = items.shape[1]
    item_blocks = items.reshape(N_COL, COL_TILES, TILE, feat_width)
    slot_index = jnp.arange(adjacency_tiles.shape[2], dtype=jnp.int32)

    def one_row(row_index):
        def add_column(running, col_index):
            slot_ids = tile_ids[row_index, col_index]
            live_mask = (slot_index < counts[row_index, col_index]).astype(jnp.float32)
            picked = item_blocks[col_index][slot_ids[1]].astype(jnp.float32)
            weights = adjacency_tiles[row_index, col_index].astype(jnp.float32)
            products = jnp.einsum("sij,sjf->sif", weights, picked) * live_mask[:, None, None]
            return running.at[slot_ids[0]].add(products), None

        start = jnp.zeros((ROW_TILES, TILE, feat_width), jnp.float32)
        running, unused = lax.scan(add_column, start, jnp.arange(N_COL, dtype=jnp.int32))
        return running

    whole = lax.map(one_row, jnp.arange(N_ROW, dtype=jnp.int32))
    return whole.reshape(N_ROW * ROW_TILES * TILE, feat_width)


def spread_items(adjacency_tiles, tile_ids, counts, users):
    feat_width = users.shape[1]
    user_blocks = users.reshape(N_ROW, ROW_TILES, TILE, feat_width)
    slot_index = jnp.arange(adjacency_tiles.shape[2], dtype=jnp.int32)

    def one_column(col_index):
        def add_row(running, row_index):
            slot_ids = tile_ids[row_index, col_index]
            live_mask = (slot_index < counts[row_index, col_index]).astype(jnp.float32)
            picked = user_blocks[row_index][slot_ids[0]].astype(jnp.float32)
            weights = adjacency_tiles[row_index, col_index].astype(jnp.float32)
            products = jnp.einsum("sji,sjf->sif", weights, picked) * live_mask[:, None, None]
            return running.at[slot_ids[1]].add(products), None

        start = jnp.zeros((COL_TILES, TILE, feat_width), jnp.float32)
        running, unused = lax.scan(add_row, start, jnp.arange(N_ROW, dtype=jnp.int32))
        return running

    whole = lax.map(one_column, jnp.arange(N_COL, dtype=jnp.int32))
    return whole.reshape(N_COL * COL_TILES * TILE, feat_width)


def reference(features, cotangent, w_first, w_second, adjacency_tiles, tile_ids, counts):
    projected = jnp.dot(features, w_first, preferred_element_type=jnp.float32).astype(jnp.bfloat16)
    z_first = spread_users(adjacency_tiles, tile_ids, counts, projected)
    gate_sig = jax.nn.sigmoid(z_first)
    hidden = (z_first * gate_sig).astype(jnp.bfloat16)
    mapped = jnp.dot(hidden, w_second, preferred_element_type=jnp.float32).astype(jnp.bfloat16)
    item_out = spread_items(adjacency_tiles, tile_ids, counts, mapped).astype(jnp.bfloat16)
    d_users = spread_users(adjacency_tiles, tile_ids, counts, cotangent).astype(jnp.bfloat16)
    grad_w2 = jnp.dot(hidden.T, d_users, preferred_element_type=jnp.float32)
    back = jnp.dot(d_users, w_second.T, preferred_element_type=jnp.float32)
    d_pre = (back * gate_sig * (1.0 + z_first * (1.0 - gate_sig))).astype(jnp.bfloat16)
    e_items = spread_items(adjacency_tiles, tile_ids, counts, d_pre).astype(jnp.bfloat16)
    grad_w1 = jnp.dot(features.T, e_items, preferred_element_type=jnp.float32)
    return (item_out, grad_w1, grad_w2)
```

```python
import jax
import jax.numpy as jnp
from jax import lax
from jax.experimental import pallas as pl
from jax.experimental.pallas import tpu as pltpu
from jax.sharding import PartitionSpec as P

TILE = 128
N_ROW = 16
N_COL = 32
SLOTS = 64
BLOCK = 1024
WIDTH = 256
USERS = BLOCK // N_COL
ITEMS = BLOCK // N_ROW
GRADS = 2 * WIDTH // N_COL
VMEM = pl.BlockSpec(memory_space=pltpu.VMEM)
SMEM = pl.BlockSpec(memory_space=pltpu.SMEM)
f32 = jnp.float32
bf16 = jnp.bfloat16


def params():
    return pltpu.CompilerParams(vmem_limit_bytes=40 * 1024 * 1024)


def cost(flops, moved):
    return pl.CostEstimate(flops=flops, bytes_accessed=moved, transcendentals=0)


def dense_kernel(ids, count, tiles, dense, turned):
    def place(k, carry):
        r = pl.multiple_of(ids[0, k] * TILE, TILE)
        c = pl.multiple_of(ids[1, k] * TILE, TILE)
        tile = jnp.where(k < count[0, 0], tiles[k], jnp.zeros((TILE, TILE), bf16))
        dense[pl.ds(r, TILE), pl.ds(c, TILE)] = tile
        turned[pl.ds(c, TILE), pl.ds(r, TILE)] = tile.T
        return carry

    lax.fori_loop(0, SLOTS, place, 0)


def make_dense(ids, count, tiles):
    shape = jax.ShapeDtypeStruct((BLOCK, BLOCK), bf16)
    return pl.pallas_call(
        dense_kernel,
        out_shape=(shape, shape),
        in_specs=[SMEM, SMEM, VMEM],
        out_specs=(VMEM, VMEM),
        compiler_params=params(),
        cost_estimate=cost(0, 3 * 2 * BLOCK * BLOCK),
        name="dense_block",
    )(ids, count, tiles)


def middle_kernel(parts, w_first, w_second, out):
    total = parts[0].astype(f32)
    for i in range(1, N_COL):
        total = total + parts[i].astype(f32)
    sums = total[:, :WIDTH]
    d_users = total[:, WIDTH:].astype(bf16)
    high = sums.astype(bf16)
    low = (sums - high.astype(f32)).astype(bf16)
    w1 = w_first[...]
    w2 = w_second[...]
    z = jnp.dot(high, w1, preferred_element_type=f32) + jnp.dot(low, w1, preferred_element_type=f32)
    s = jax.nn.sigmoid(z)
    hidden = (z * s).astype(bf16)
    mapped = jnp.dot(hidden, w2, preferred_element_type=f32).astype(bf16)
    back = lax.dot_general(d_users, w2, (((1,), (1,)), ((), ())), preferred_element_type=f32)
    d_pre = (back * s * (1.0 + z * (1.0 - s))).astype(bf16)
    over_users = (((0,), (0,)), ((), ()))
    grad_one = lax.dot_general(high, d_pre, over_users, preferred_element_type=f32) + lax.dot_general(
        low, d_pre, over_users, preferred_element_type=f32
    )
    grad_two = lax.dot_general(hidden, d_users, over_users, preferred_element_type=f32)
    half = GRADS // 2
    for i in range(N_COL):
        out[i, :USERS] = mapped
        both = jnp.concatenate([grad_one[i * half : (i + 1) * half], grad_two[i * half : (i + 1) * half]], axis=0)
        out[i, USERS:] = both.astype(bf16)


def middle(parts, w_first, w_second):
    return pl.pallas_call(
        middle_kernel,
        out_shape=jax.ShapeDtypeStruct((N_COL, USERS + GRADS, WIDTH), bf16),
        in_specs=[VMEM, VMEM, VMEM],
        out_specs=VMEM,
        compiler_params=params(),
        name="middle",
    )(parts, w_first, w_second)


def back_kernel(got, turned, out, mapped):
    grads = got[0, USERS:].astype(f32)
    for i in range(1, N_COL):
        grads = grads + got[i, USERS:].astype(f32)
    for i in range(N_COL):
        mapped[i * USERS : (i + 1) * USERS] = got[i, :USERS]
    grads = grads.astype(bf16)
    for i in range(N_ROW):
        out[i, ITEMS:] = grads
    per = 4
    rows = per * ITEMS
    for i in range(N_ROW // per):
        part = jnp.dot(turned[i * rows : (i + 1) * rows], mapped[...], preferred_element_type=f32).astype(bf16)
        for j in range(per):
            out[i * per + j, :ITEMS] = part[j * ITEMS : (j + 1) * ITEMS]


def back_product(got, turned):
    return pl.pallas_call(
        back_kernel,
        out_shape=jax.ShapeDtypeStruct((N_ROW, ITEMS + GRADS, WIDTH), bf16),
        in_specs=[VMEM, VMEM],
        out_specs=VMEM,
        scratch_shapes=[pltpu.VMEM((BLOCK, WIDTH), bf16)],
        compiler_params=params(),
        name="back_product",
    )(got, turned)


def shards(features, cotangent, w_first, w_second, adjacency_tiles, tile_ids, counts):
    both = jnp.concatenate([features, cotangent], axis=1)
    spread = jnp.broadcast_to(both[None], (N_ROW, ITEMS, 2 * WIDTH))
    dense, turned = make_dense(tile_ids[0, 0], counts, adjacency_tiles[0, 0])
    items = lax.all_to_all(spread, "row", 0, 0).reshape(BLOCK, 2 * WIDTH)
    partial = jnp.dot(dense, items, preferred_element_type=f32).astype(bf16)
    parts = lax.all_to_all(partial.reshape(N_COL, USERS, 2 * WIDTH), "col", 0, 0)
    sent = middle(parts, w_first, w_second)
    got = lax.all_to_all(sent, "col", 0, 0)
    sent = back_product(got, turned)
    got = lax.all_to_all(sent, "row", 0, 0)
    grads = jnp.sum(got[:, ITEMS:].astype(f32), axis=0).astype(bf16)
    item_out = jnp.sum(got[:, :ITEMS].astype(f32), axis=0).astype(bf16)
    grads = lax.all_to_all(jnp.broadcast_to(grads[None], (N_COL, GRADS, WIDTH)), "col", 0, 0)
    half = GRADS // 2
    grad_one = grads[:, :half].astype(f32).reshape(WIDTH, WIDTH)
    grad_two = grads[:, half:].astype(f32).reshape(WIDTH, WIDTH)
    return (item_out, grad_one, grad_two)


def solution(mesh):
    return jax.shard_map(
        shards,
        mesh=mesh,
        in_specs=(
            P(("col", "row"), None),
            P(("col", "row"), None),
            P(),
            P(),
            P("row", "col", None, None, None),
            P("row", "col", None, None),
            P("row", "col"),
        ),
        out_specs=(P(("col", "row"), None), P(), P()),
        check_vma=False,
    )
```

```python
import jax
import jax.numpy as jnp
from jax import lax
from jax.experimental import pallas as pl
from jax.experimental.pallas import tpu as pltpu
from jax.sharding import PartitionSpec as P

TILE = 128
N_ROW = 16
N_COL = 32
SLOTS = 64
BLOCK = 1024
WIDTH = 256
USERS = BLOCK // N_COL
ITEMS = BLOCK // N_ROW
GRADS = 2 * WIDTH // N_COL
PEERS = N_COL // 2
HALF = BLOCK // 2
VMEM = pl.BlockSpec(memory_space=pltpu.VMEM)
SMEM = pl.BlockSpec(memory_space=pltpu.SMEM)
f32 = jnp.float32
bf16 = jnp.bfloat16


def params():
    return pltpu.CompilerParams(vmem_limit_bytes=40 * 1024 * 1024)


def cost(flops, moved):
    return pl.CostEstimate(flops=flops, bytes_accessed=moved, transcendentals=0)


def spread_kernel(features, cotangent, out):
    for i in range(N_ROW):
        out[i, :, :WIDTH] = features[...]
        out[i, :, WIDTH:] = cotangent[...]


def spread_items(features, cotangent):
    return pl.pallas_call(
        spread_kernel,
        out_shape=jax.ShapeDtypeStruct((N_ROW, ITEMS, 2 * WIDTH), bf16),
        in_specs=[VMEM, VMEM],
        out_specs=VMEM,
        compiler_params=params(),
        name="spread_items",
    )(features, cotangent)


def dense_kernel(core, ids, count, tiles, dense, turned):
    mine = core[0, 0]

    def place(k, carry):
        r = ids[0, k]
        c = pl.multiple_of(ids[1, k] * TILE, TILE)
        tile = jnp.where(k < count[0, 0], tiles[k], jnp.zeros((TILE, TILE), bf16))
        for part in range(TILE // USERS):
            half = lax.rem(part + mine, 2)
            row = pl.multiple_of(r * (TILE // 2) + part // 2 * USERS, USERS)
            dense[half, pl.ds(row, USERS), pl.ds(c, TILE)] = tile[part * USERS : (part + 1) * USERS]
        turned[pl.ds(c, TILE), pl.ds(pl.multiple_of(r * TILE, TILE), TILE)] = tile.T
        return carry

    lax.fori_loop(0, SLOTS, place, 0)


def make_dense(core, ids, count, tiles):
    return pl.pallas_call(
        dense_kernel,
        out_shape=(
            jax.ShapeDtypeStruct((2, HALF, BLOCK), bf16),
            jax.ShapeDtypeStruct((BLOCK, BLOCK), bf16),
        ),
        in_specs=[SMEM, SMEM, SMEM, VMEM],
        out_specs=(VMEM, VMEM),
        compiler_params=params(),
        cost_estimate=cost(0, 3 * 2 * BLOCK * BLOCK),
        name="dense_block",
    )(core, ids, count, tiles)


CHUNK = 256


def theirs_kernel(dense, items, out):
    for i in range(0, HALF, CHUNK):
        out[i : i + CHUNK] = jnp.dot(dense[1, i : i + CHUNK], items[...], preferred_element_type=f32).astype(bf16)


def mine_kernel(dense, items, other, out):
    for i in range(0, HALF, CHUNK):
        part = jnp.dot(dense[0, i : i + CHUNK], items[...], preferred_element_type=f32)
        out[i : i + CHUNK] = (part + other[i : i + CHUNK].astype(f32)).astype(bf16)


def half_product(kernel, *operands):
    return pl.pallas_call(
        kernel,
        out_shape=jax.ShapeDtypeStruct((HALF, 2 * WIDTH), bf16),
        in_specs=[VMEM] * len(operands),
        out_specs=VMEM,
        compiler_params=params(),
        cost_estimate=cost(2 * HALF * BLOCK * 2 * WIDTH, 3 * 1024 * 1024),
        name="user_product",
    )(*operands)


def middle_kernel(parts, w_first, w_second, out):
    total = parts[0].astype(f32)
    for i in range(1, PEERS):
        total = total + parts[i].astype(f32)
    sums = total[:, :WIDTH]
    d_users = total[:, WIDTH:].astype(bf16)
    high = sums.astype(bf16)
    low = (sums - high.astype(f32)).astype(bf16)
    w1 = w_first[...]
    w2 = w_second[...]
    z = jnp.dot(high, w1, preferred_element_type=f32) + jnp.dot(low, w1, preferred_element_type=f32)
    s = jax.nn.sigmoid(z)
    hidden = (z * s).astype(bf16)
    mapped = jnp.dot(hidden, w2, preferred_element_type=f32).astype(bf16)
    back = lax.dot_general(d_users, w2, (((1,), (1,)), ((), ())), preferred_element_type=f32)
    d_pre = (back * s * (1.0 + z * (1.0 - s))).astype(bf16)
    over_users = (((0,), (0,)), ((), ()))
    grad_one = lax.dot_general(high, d_pre, over_users, preferred_element_type=f32) + lax.dot_general(
        low, d_pre, over_users, preferred_element_type=f32
    )
    grad_two = lax.dot_general(hidden, d_users, over_users, preferred_element_type=f32)
    half = GRADS // 2
    for i in range(PEERS):
        out[i, :USERS] = mapped
        for k in range(2):
            rows = slice((2 * i + k) * half, (2 * i + k + 1) * half)
            both = jnp.concatenate([grad_one[rows], grad_two[rows]], axis=0)
            out[i, USERS + k * GRADS : USERS + (k + 1) * GRADS] = both.astype(bf16)


def middle(parts, w_first, w_second):
    return pl.pallas_call(
        middle_kernel,
        out_shape=jax.ShapeDtypeStruct((PEERS, USERS + 2 * GRADS, WIDTH), bf16),
        in_specs=[VMEM, VMEM, VMEM],
        out_specs=VMEM,
        compiler_params=params(),
        name="middle",
    )(parts, w_first, w_second)


def back_kernel(core, got, other, turned, out, mapped):
    mine = core[0, 0]
    slot = pl.multiple_of(USERS + mine * GRADS, GRADS)
    grads = jnp.zeros((GRADS, WIDTH), f32)
    for i in range(PEERS):
        grads = grads + got[i, pl.ds(slot, GRADS)].astype(f32) + other[i, pl.ds(slot, GRADS)].astype(f32)
        mapped[pl.ds(pl.multiple_of((2 * i + mine) * USERS, USERS), USERS)] = got[i, :USERS]
        mapped[pl.ds(pl.multiple_of((2 * i + 1 - mine) * USERS, USERS), USERS)] = other[i, :USERS]
    grads = grads.astype(bf16)
    for i in range(N_ROW):
        out[i, ITEMS:] = grads
    per = CHUNK // ITEMS
    for i in range(N_ROW // per):
        part = jnp.dot(turned[i * CHUNK : (i + 1) * CHUNK], mapped[...], preferred_element_type=f32).astype(bf16)
        for j in range(per):
            out[i * per + j, :ITEMS] = part[j * ITEMS : (j + 1) * ITEMS]


def back_product(core, got, other, turned):
    return pl.pallas_call(
        back_kernel,
        out_shape=jax.ShapeDtypeStruct((N_ROW, ITEMS + GRADS, WIDTH), bf16),
        in_specs=[SMEM, VMEM, VMEM, VMEM],
        out_specs=VMEM,
        scratch_shapes=[pltpu.VMEM((BLOCK, WIDTH), bf16)],
        compiler_params=params(),
        name="back_product",
    )(core, got, other, turned)


def shards(features, cotangent, w_first, w_second, adjacency_tiles, tile_ids, counts):
    core = lax.rem(lax.axis_index("col"), 2).reshape(1, 1)
    same_core = [[2 * i + k for i in range(PEERS)] for k in range(2)]
    swap = [(i, i ^ 1) for i in range(N_COL)]
    spread = spread_items(features, cotangent)
    dense, turned = make_dense(core, tile_ids[0, 0], counts, adjacency_tiles[0, 0])
    items = lax.all_to_all(spread, "row", 0, 0).reshape(BLOCK, 2 * WIDTH)
    other = lax.ppermute(half_product(theirs_kernel, dense, items), "col", swap)
    sums = half_product(mine_kernel, dense, items, other).reshape(PEERS, USERS, 2 * WIDTH)
    parts = lax.all_to_all(sums, "col", 0, 0, axis_index_groups=same_core)
    sent = middle(parts, w_first, w_second)
    got = lax.all_to_all(sent, "col", 0, 0, axis_index_groups=same_core)
    other = lax.ppermute(got, "col", swap)
    sent = back_product(core, got, other, turned)
    got = lax.all_to_all(sent, "row", 0, 0)
    grads = jnp.sum(got[:, ITEMS:].astype(f32), axis=0).astype(bf16)
    item_out = jnp.sum(got[:, :ITEMS].astype(f32), axis=0).astype(bf16)
    grads = lax.all_to_all(jnp.broadcast_to(grads[None], (N_COL, GRADS, WIDTH)), "col", 0, 0)
    half = GRADS // 2
    grad_one = grads[:, :half].astype(f32).reshape(WIDTH, WIDTH)
    grad_two = grads[:, half:].astype(f32).reshape(WIDTH, WIDTH)
    return (item_out, grad_one, grad_two)


def solution(mesh):
    return jax.shard_map(
        shards,
        mesh=mesh,
        in_specs=(
            P(("col", "row"), None),
            P(("col", "row"), None),
            P(),
            P(),
            P("row", "col", None, None, None),
            P("row", "col", None, None),
            P("row", "col"),
        ),
        out_specs=(P(("col", "row"), None), P(), P()),
        check_vma=False,
    )
```

```python
import jax
import jax.numpy as jnp
from jax import lax
from jax.experimental import pallas as pl
from jax.experimental.pallas import tpu as pltpu
from jax.sharding import PartitionSpec as P

TILE = 128
N_ROW = 16
N_COL = 32
SLOTS = 64
BLOCK = 1024
WIDTH = 256
USERS = BLOCK // N_COL
ITEMS = BLOCK // N_ROW
GRADS = 2 * WIDTH // N_COL
PEERS = N_COL // 2
NEAR = 4
HALF = BLOCK // 2
VMEM = pl.BlockSpec(memory_space=pltpu.VMEM)
ANY = pl.BlockSpec(memory_space=pl.ANY)
SMEM = pl.BlockSpec(memory_space=pltpu.SMEM)
f32 = jnp.float32
bf16 = jnp.bfloat16


def params(mib=24):
    return pltpu.CompilerParams(vmem_limit_bytes=mib * 1024 * 1024)


def cost(flops, moved):
    return pl.CostEstimate(flops=flops, bytes_accessed=moved, transcendentals=0)


def held(array):
    return pltpu.with_memory_space_constraint(array, pltpu.HBM)


def first_kernel(features, cotangent, out, both, in_sems, out_sems):
    loads = [
        pltpu.make_async_copy(features, both.at[:, :WIDTH], in_sems.at[0]),
        pltpu.make_async_copy(cotangent, both.at[:, WIDTH:], in_sems.at[1]),
    ]
    for copy in loads:
        copy.start()
    for copy in loads:
        copy.wait()
    stores = [pltpu.make_async_copy(both, out.at[i], out_sems.at[i]) for i in range(NEAR)]
    for copy in stores:
        copy.start()
    for copy in stores:
        copy.wait()


def first_spread(features, cotangent):
    return pl.pallas_call(
        first_kernel,
        out_shape=jax.ShapeDtypeStruct((NEAR, ITEMS, 2 * WIDTH), bf16),
        in_specs=[ANY, ANY],
        out_specs=ANY,
        scratch_shapes=[
            pltpu.VMEM((ITEMS, 2 * WIDTH), bf16),
            pltpu.SemaphoreType.DMA((2,)),
            pltpu.SemaphoreType.DMA((NEAR,)),
        ],
        compiler_params=params(),
        cost_estimate=cost(0, 2 * NEAR * ITEMS * 4 * WIDTH),
        name="first_spread",
    )(held(features), held(cotangent))


def second_kernel(rows, after, out):
    for i in range(NEAR):
        out[i] = rows[...]


def second_spread(rows, after):
    return pl.pallas_call(
        second_kernel,
        out_shape=jax.ShapeDtypeStruct((NEAR,) + rows.shape, bf16),
        in_specs=[VMEM, ANY],
        out_specs=VMEM,
        compiler_params=params(),
        name="second_spread",
    )(rows, after)


LOADS = 8
LOAD = SLOTS // LOADS


def dense_kernel(core, ids, count, tiles, dense, turned, held, sems):
    mine = core[0, 0]
    copies = []
    for i in range(LOADS):
        part = pl.ds(i * LOAD, LOAD)
        copies.append(pltpu.make_async_copy(tiles.at[part], held.at[part], sems.at[i]))
    for copy in copies:
        copy.start()
    for i in range(LOADS):
        copies[i].wait()
        for k in range(i * LOAD, (i + 1) * LOAD):
            r = ids[0, k]
            c = pl.multiple_of(ids[1, k] * TILE, TILE)
            tile = jnp.where(k < count[0, 0], held[k], jnp.zeros((TILE, TILE), bf16))
            for part in range(TILE // USERS):
                half = lax.rem(part + mine, 2)
                row = pl.multiple_of(r * (TILE // 2) + part // 2 * USERS, USERS)
                dense[half, pl.ds(row, USERS), pl.ds(c, TILE)] = tile[part * USERS : (part + 1) * USERS]
            turned[pl.ds(c, TILE), pl.ds(pl.multiple_of(r * TILE, TILE), TILE)] = tile.T


def make_dense(core, ids, count, tiles):
    return pl.pallas_call(
        dense_kernel,
        out_shape=(
            jax.ShapeDtypeStruct((2, HALF, BLOCK), bf16),
            jax.ShapeDtypeStruct((BLOCK, BLOCK), bf16),
        ),
        in_specs=[SMEM, SMEM, SMEM, ANY],
        out_specs=(VMEM, VMEM),
        scratch_shapes=[pltpu.VMEM((SLOTS, TILE, TILE), bf16), pltpu.SemaphoreType.DMA((LOADS,))],
        compiler_params=params(),
        cost_estimate=cost(0, 3 * 2 * BLOCK * BLOCK),
        name="dense_block",
    )(core, ids, count, held(tiles))


CHUNK = 256


def theirs_kernel(dense, items, out):
    for i in range(0, HALF, CHUNK):
        out[i : i + CHUNK] = jnp.dot(dense[1, i : i + CHUNK], items[...], preferred_element_type=f32).astype(bf16)


def mine_kernel(dense, items, other, out):
    for i in range(0, HALF, CHUNK):
        part = jnp.dot(dense[0, i : i + CHUNK], items[...], preferred_element_type=f32)
        out[i : i + CHUNK] = (part + other[i : i + CHUNK].astype(f32)).astype(bf16)


def half_product(kernel, *operands):
    return pl.pallas_call(
        kernel,
        out_shape=jax.ShapeDtypeStruct((HALF, 2 * WIDTH), bf16),
        in_specs=[VMEM] * len(operands),
        out_specs=VMEM,
        compiler_params=params(),
        cost_estimate=cost(2 * HALF * BLOCK * 2 * WIDTH, 3 * 1024 * 1024),
        name="user_product",
    )(*operands)


def middle_kernel(parts, w_first, w_second, out):
    total = parts[0].astype(f32)
    for i in range(1, PEERS):
        total = total + parts[i].astype(f32)
    sums = total[:, :WIDTH]
    d_users = total[:, WIDTH:].astype(bf16)
    high = sums.astype(bf16)
    low = (sums - high.astype(f32)).astype(bf16)
    w1 = w_first[...]
    w2 = w_second[...]
    z = jnp.dot(high, w1, preferred_element_type=f32) + jnp.dot(low, w1, preferred_element_type=f32)
    s = jax.nn.sigmoid(z)
    hidden = (z * s).astype(bf16)
    mapped = jnp.dot(hidden, w2, preferred_element_type=f32).astype(bf16)
    back = lax.dot_general(d_users, w2, (((1,), (1,)), ((), ())), preferred_element_type=f32)
    d_pre = (back * s * (1.0 + z * (1.0 - s))).astype(bf16)
    over_users = (((0,), (0,)), ((), ()))
    grad_one = lax.dot_general(high, d_pre, over_users, preferred_element_type=f32) + lax.dot_general(
        low, d_pre, over_users, preferred_element_type=f32
    )
    grad_two = lax.dot_general(hidden, d_users, over_users, preferred_element_type=f32)
    half = GRADS // 2
    for i in range(PEERS):
        out[i, :USERS] = mapped
        for k in range(2):
            rows = slice((2 * i + k) * half, (2 * i + k + 1) * half)
            both = jnp.concatenate([grad_one[rows], grad_two[rows]], axis=0)
            out[i, USERS + k * GRADS : USERS + (k + 1) * GRADS] = both.astype(bf16)


def middle(parts, w_first, w_second):
    return pl.pallas_call(
        middle_kernel,
        out_shape=jax.ShapeDtypeStruct((PEERS, USERS + 2 * GRADS, WIDTH), bf16),
        in_specs=[VMEM, VMEM, VMEM],
        out_specs=VMEM,
        compiler_params=params(),
        name="middle",
    )(parts, w_first, w_second)


def back_kernel(core, got, other, turned, out, mapped):
    mine = core[0, 0]
    slot = pl.multiple_of(USERS + mine * GRADS, GRADS)
    grads = jnp.zeros((GRADS, WIDTH), f32)
    for i in range(PEERS):
        grads = grads + got[i, pl.ds(slot, GRADS)].astype(f32) + other[i, pl.ds(slot, GRADS)].astype(f32)
        mapped[pl.ds(pl.multiple_of((2 * i + mine) * USERS, USERS), USERS)] = got[i, :USERS]
        mapped[pl.ds(pl.multiple_of((2 * i + 1 - mine) * USERS, USERS), USERS)] = other[i, :USERS]
    grads = grads.astype(bf16)
    for i in range(N_ROW):
        out[i, ITEMS:] = grads
    per = CHUNK // ITEMS
    for i in range(N_ROW // per):
        part = jnp.dot(turned[i * CHUNK : (i + 1) * CHUNK], mapped[...], preferred_element_type=f32).astype(bf16)
        for j in range(per):
            out[i * per + j, :ITEMS] = part[j * ITEMS : (j + 1) * ITEMS]


def back_product(core, got, other, turned):
    return pl.pallas_call(
        back_kernel,
        out_shape=jax.ShapeDtypeStruct((N_ROW, ITEMS + GRADS, WIDTH), bf16),
        in_specs=[SMEM, VMEM, VMEM, VMEM],
        out_specs=VMEM,
        scratch_shapes=[pltpu.VMEM((BLOCK, WIDTH), bf16)],
        compiler_params=params(),
        name="back_product",
    )(core, got, other, turned)


def last_kernel(got, out):
    grads = got[0, ITEMS:].astype(f32)
    for i in range(1, N_ROW):
        grads = grads + got[i, ITEMS:].astype(f32)
    grads = grads.astype(bf16)
    for i in range(N_COL):
        out[i] = grads


def last_spread(got):
    return pl.pallas_call(
        last_kernel,
        out_shape=jax.ShapeDtypeStruct((N_COL, GRADS, WIDTH), bf16),
        in_specs=[VMEM],
        out_specs=VMEM,
        compiler_params=params(),
        name="last_spread",
    )(got)


def shards(features, cotangent, w_first, w_second, adjacency_tiles, tile_ids, counts):
    core = lax.rem(lax.axis_index("col"), 2).reshape(1, 1)
    same_core = [[2 * i + k for i in range(PEERS)] for k in range(2)]
    swap = [(i, i ^ 1) for i in range(N_COL)]
    same_x = [[NEAR * i + k for k in range(NEAR)] for i in range(NEAR)]
    same_z = [[NEAR * i + k for i in range(NEAR)] for k in range(NEAR)]
    spread = first_spread(features, cotangent)
    dense, turned = make_dense(core, tile_ids[0, 0], counts, adjacency_tiles[0, 0])
    items = lax.all_to_all(spread, "row", 0, 0, axis_index_groups=same_x).reshape(NEAR * ITEMS, 2 * WIDTH)
    items = lax.all_to_all(second_spread(items, dense), "row", 0, 0, axis_index_groups=same_z).reshape(BLOCK, 2 * WIDTH)
    other = lax.ppermute(half_product(theirs_kernel, dense, items), "col", swap)
    sums = half_product(mine_kernel, dense, items, other).reshape(PEERS, USERS, 2 * WIDTH)
    parts = lax.all_to_all(sums, "col", 0, 0, axis_index_groups=same_core)
    sent = middle(parts, w_first, w_second)
    got = lax.all_to_all(sent, "col", 0, 0, axis_index_groups=same_core)
    other = lax.ppermute(got, "col", swap)
    sent = back_product(core, got, other, turned)
    got = lax.all_to_all(sent, "row", 0, 0)
    item_out = jnp.sum(got[:, :ITEMS].astype(f32), axis=0).astype(bf16)
    grads = lax.all_to_all(last_spread(got), "col", 0, 0)
    half = GRADS // 2
    grad_one = grads[:, :half].astype(f32).reshape(WIDTH, WIDTH)
    grad_two = grads[:, half:].astype(f32).reshape(WIDTH, WIDTH)
    return (item_out, grad_one, grad_two)


def solution(mesh):
    return jax.shard_map(
        shards,
        mesh=mesh,
        in_specs=(
            P(("col", "row"), None),
            P(("col", "row"), None),
            P(),
            P(),
            P("row", "col", None, None, None),
            P("row", "col", None, None),
            P("row", "col"),
        ),
        out_specs=(P(("col", "row"), None), P(), P()),
        check_vma=False,
    )
```

```python
import jax
import jax.numpy as jnp
from jax import lax
from jax.experimental import pallas as pl
from jax.experimental.pallas import tpu as pltpu
from jax.sharding import PartitionSpec as P

TILE = 128
N_ROW = 16
N_COL = 32
SLOTS = 64
BLOCK = 1024
WIDTH = 256
USERS = BLOCK // N_COL
ITEMS = BLOCK // N_ROW
GRADS = 2 * WIDTH // N_COL
PEERS = N_COL // 2
NEAR = 4
RING = (0, 7, 1, 6, 2, 5, 3, 4)
COLS = tuple(2 * y + half for half in range(2) for y in RING)
HALF = BLOCK // 2
VMEM = pl.BlockSpec(memory_space=pltpu.VMEM)
ANY = pl.BlockSpec(memory_space=pl.ANY)
SMEM = pl.BlockSpec(memory_space=pltpu.SMEM)
f32 = jnp.float32
bf16 = jnp.bfloat16


def params(mib=24):
    return pltpu.CompilerParams(vmem_limit_bytes=mib * 1024 * 1024)


def cost(flops, moved):
    return pl.CostEstimate(flops=flops, bytes_accessed=moved, transcendentals=0)


def held(array):
    return pltpu.with_memory_space_constraint(array, pltpu.HBM)


def first_kernel(features, cotangent, out, both, in_sems, out_sems):
    loads = [
        pltpu.make_async_copy(features, both.at[:, :WIDTH], in_sems.at[0]),
        pltpu.make_async_copy(cotangent, both.at[:, WIDTH:], in_sems.at[1]),
    ]
    for copy in loads:
        copy.start()
    for copy in loads:
        copy.wait()
    stores = [pltpu.make_async_copy(both, out.at[i], out_sems.at[i]) for i in range(NEAR)]
    for copy in stores:
        copy.start()
    for copy in stores:
        copy.wait()


def first_spread(features, cotangent):
    return pl.pallas_call(
        first_kernel,
        out_shape=jax.ShapeDtypeStruct((NEAR, ITEMS, 2 * WIDTH), bf16),
        in_specs=[ANY, ANY],
        out_specs=ANY,
        scratch_shapes=[
            pltpu.VMEM((ITEMS, 2 * WIDTH), bf16),
            pltpu.SemaphoreType.DMA((2,)),
            pltpu.SemaphoreType.DMA((NEAR,)),
        ],
        compiler_params=params(),
        cost_estimate=cost(0, 2 * NEAR * ITEMS * 4 * WIDTH),
        name="first_spread",
    )(held(features), held(cotangent))


def second_kernel(rows, after, out):
    for i in range(NEAR):
        out[i] = rows[...]


def second_spread(rows, after):
    return pl.pallas_call(
        second_kernel,
        out_shape=jax.ShapeDtypeStruct((NEAR,) + rows.shape, bf16),
        in_specs=[VMEM, ANY],
        out_specs=VMEM,
        compiler_params=params(),
        name="second_spread",
    )(rows, after)


LOADS = 8
LOAD = SLOTS // LOADS


def dense_kernel(core, count, ids_hbm, tiles, dense, fetched, ids, sems, ids_sem):
    mine = core[0, 0]
    ids_copy = pltpu.make_async_copy(ids_hbm, ids, ids_sem)
    ids_copy.start()
    copies = []
    for i in range(LOADS):
        part = pl.ds(i * LOAD, LOAD)
        copies.append(pltpu.make_async_copy(tiles.at[part], fetched.at[part], sems.at[i]))
    for copy in copies:
        copy.start()
    ids_copy.wait()
    for i in range(LOADS):
        copies[i].wait()
        for k in range(i * LOAD, (i + 1) * LOAD):
            r = ids[0, k]
            c = pl.multiple_of(ids[1, k] * TILE, TILE)
            tile = jnp.where(k < count[0, 0], fetched[k], jnp.zeros((TILE, TILE), bf16))
            place = jnp.where(r < NEAR, 2 * r, 15 - 2 * r)
            for part in range(TILE // USERS):
                half = lax.rem(part + mine, 2)
                row = pl.multiple_of((place + part // 2 * (PEERS // 2)) * USERS, USERS)
                dense[half, pl.ds(row, USERS), pl.ds(c, TILE)] = tile[part * USERS : (part + 1) * USERS]


def make_dense(core, ids, count, tiles):
    return pl.pallas_call(
        dense_kernel,
        out_shape=jax.ShapeDtypeStruct((2, HALF, BLOCK), bf16),
        in_specs=[SMEM, SMEM, ANY, ANY],
        out_specs=VMEM,
        scratch_shapes=[
            pltpu.VMEM((SLOTS, TILE, TILE), bf16),
            pltpu.SMEM((2, SLOTS), jnp.int32),
            pltpu.SemaphoreType.DMA((LOADS,)),
            pltpu.SemaphoreType.DMA,
        ],
        compiler_params=params(),
        cost_estimate=cost(0, 3 * 2 * BLOCK * BLOCK),
        name="dense_block",
    )(core, count, held(ids), held(tiles))


def turn_kernel(dense, after, turned):
    for half in range(2):
        for i in range(0, HALF, TILE):
            for j in range(0, BLOCK, TILE):
                turned[j : j + TILE, half * HALF + i : half * HALF + i + TILE] = dense[half, i : i + TILE, j : j + TILE].T


def turn(dense, after):
    return pl.pallas_call(
        turn_kernel,
        out_shape=jax.ShapeDtypeStruct((BLOCK, BLOCK), bf16),
        in_specs=[VMEM, ANY],
        out_specs=VMEM,
        compiler_params=params(),
        cost_estimate=cost(0, 4 * BLOCK * BLOCK),
        name="turned_block",
    )(dense, after)


CHUNK = 256


def theirs_kernel(dense, items, out):
    for i in range(0, HALF, CHUNK):
        out[i : i + CHUNK] = jnp.dot(dense[1, i : i + CHUNK], items[...], preferred_element_type=f32).astype(bf16)


def mine_kernel(dense, items, out):
    for i in range(0, HALF, CHUNK):
        out[i : i + CHUNK] = jnp.dot(dense[0, i : i + CHUNK], items[...], preferred_element_type=f32)


def add_kernel(mine, other, out):
    out[...] = (mine[...] + other[...].astype(f32)).astype(bf16)


def half_product(kernel, dtype, *operands):
    return pl.pallas_call(
        kernel,
        out_shape=jax.ShapeDtypeStruct((HALF, 2 * WIDTH), dtype),
        in_specs=[VMEM] * len(operands),
        out_specs=VMEM,
        compiler_params=params(),
        cost_estimate=cost(2 * HALF * BLOCK * 2 * WIDTH, 3 * 1024 * 1024),
        name="user_product",
    )(*operands)


def middle_kernel(parts, w_first, w_second, out):
    total = parts[0].astype(f32)
    for i in range(1, PEERS):
        total = total + parts[i].astype(f32)
    sums = total[:, :WIDTH]
    d_users = total[:, WIDTH:].astype(bf16)
    high = sums.astype(bf16)
    low = (sums - high.astype(f32)).astype(bf16)
    w1 = w_first[...]
    w2 = w_second[...]
    z = jnp.dot(high, w1, preferred_element_type=f32) + jnp.dot(low, w1, preferred_element_type=f32)
    s = jax.nn.sigmoid(z)
    hidden = (z * s).astype(bf16)
    mapped = jnp.dot(hidden, w2, preferred_element_type=f32).astype(bf16)
    back = lax.dot_general(d_users, w2, (((1,), (1,)), ((), ())), preferred_element_type=f32)
    d_pre = (back * s * (1.0 + z * (1.0 - s))).astype(bf16)
    over_users = (((0,), (0,)), ((), ()))
    grad_one = lax.dot_general(high, d_pre, over_users, preferred_element_type=f32) + lax.dot_general(
        low, d_pre, over_users, preferred_element_type=f32
    )
    grad_two = lax.dot_general(hidden, d_users, over_users, preferred_element_type=f32)
    half = GRADS // 2
    for i in range(PEERS):
        out[i, :USERS] = mapped
        for k in range(2):
            rows = slice((2 * COLS[i] + k) * half, (2 * COLS[i] + k + 1) * half)
            both = jnp.concatenate([grad_one[rows], grad_two[rows]], axis=0)
            out[i, USERS + k * GRADS : USERS + (k + 1) * GRADS] = both.astype(bf16)


def middle(parts, w_first, w_second):
    return pl.pallas_call(
        middle_kernel,
        out_shape=jax.ShapeDtypeStruct((PEERS, USERS + 2 * GRADS, WIDTH), bf16),
        in_specs=[VMEM, VMEM, VMEM],
        out_specs=VMEM,
        compiler_params=params(),
        name="middle",
    )(parts, w_first, w_second)


def own_kernel(got, turned, out, mapped):
    for i in range(PEERS):
        mapped[i * USERS : (i + 1) * USERS] = got[i, :USERS]
    for i in range(0, BLOCK, CHUNK):
        out[i : i + CHUNK] = jnp.dot(turned[i : i + CHUNK, :HALF], mapped[...], preferred_element_type=f32)


def own_product(got, turned):
    return pl.pallas_call(
        own_kernel,
        out_shape=jax.ShapeDtypeStruct((BLOCK, WIDTH), f32),
        in_specs=[VMEM, VMEM],
        out_specs=VMEM,
        scratch_shapes=[pltpu.VMEM((HALF, WIDTH), bf16)],
        compiler_params=params(),
        cost_estimate=cost(2 * BLOCK * HALF * WIDTH, 3 * 1024 * 1024),
        name="own_product",
    )(got, turned)


def back_kernel(core, got, other, own, turned, out, mapped):
    slot = pl.multiple_of(USERS + core[0, 0] * GRADS, GRADS)
    grads = jnp.zeros((GRADS, WIDTH), f32)
    for i in range(PEERS):
        grads = grads + got[i, pl.ds(slot, GRADS)].astype(f32) + other[i, pl.ds(slot, GRADS)].astype(f32)
        mapped[i * USERS : (i + 1) * USERS] = other[i, :USERS]
    grads = grads.astype(bf16)
    for i in range(N_ROW):
        out[i, ITEMS:] = grads
    per = CHUNK // ITEMS
    for i in range(N_ROW // per):
        rows = slice(i * CHUNK, (i + 1) * CHUNK)
        part = own[rows] + jnp.dot(turned[rows, HALF:], mapped[...], preferred_element_type=f32)
        part = part.astype(bf16)
        for j in range(per):
            out[i * per + j, :ITEMS] = part[j * ITEMS : (j + 1) * ITEMS]


def back_product(core, got, other, own, turned):
    return pl.pallas_call(
        back_kernel,
        out_shape=jax.ShapeDtypeStruct((N_ROW, ITEMS + GRADS, WIDTH), bf16),
        in_specs=[SMEM, VMEM, VMEM, VMEM, VMEM],
        out_specs=VMEM,
        scratch_shapes=[pltpu.VMEM((HALF, WIDTH), bf16)],
        compiler_params=params(),
        name="back_product",
    )(core, got, other, own, turned)


def last_kernel(got, out):
    grads = got[0, ITEMS:].astype(f32)
    for i in range(1, N_ROW):
        grads = grads + got[i, ITEMS:].astype(f32)
    grads = grads.astype(bf16)
    for i in range(N_COL):
        out[i] = grads


def last_spread(got):
    return pl.pallas_call(
        last_kernel,
        out_shape=jax.ShapeDtypeStruct((N_COL, GRADS, WIDTH), bf16),
        in_specs=[VMEM],
        out_specs=VMEM,
        compiler_params=params(),
        name="last_spread",
    )(got)


def shards(features, cotangent, w_first, w_second, adjacency_tiles, tile_ids, counts):
    core = lax.rem(lax.axis_index("col"), 2).reshape(1, 1)
    same_core = [[2 * i + k for i in COLS] for k in range(2)]
    same_x = [[NEAR * i + k for k in range(NEAR)] for i in range(NEAR)]
    same_z = [[NEAR * i + k for i in range(NEAR)] for k in range(NEAR)]
    swap = [(i, i ^ 1) for i in range(N_COL)]
    spread = first_spread(features, cotangent)
    dense = make_dense(core, tile_ids[0, 0], counts, adjacency_tiles[0, 0])
    items = lax.all_to_all(spread, "row", 0, 0, axis_index_groups=same_x).reshape(NEAR * ITEMS, 2 * WIDTH)
    items = lax.all_to_all(second_spread(items, dense), "row", 0, 0, axis_index_groups=same_z)
    items = items.reshape(BLOCK, 2 * WIDTH)
    theirs = half_product(theirs_kernel, bf16, dense, items)
    other = lax.ppermute(theirs, "col", swap)
    mine = half_product(mine_kernel, f32, dense, items)
    turned = turn(dense, theirs)
    sums = half_product(add_kernel, bf16, mine, other).reshape(PEERS, USERS, 2 * WIDTH)
    parts = lax.all_to_all(sums, "col", 0, 0, axis_index_groups=same_core)
    sent = middle(parts, w_first, w_second)
    got = lax.all_to_all(sent, "col", 0, 0, axis_index_groups=same_core)
    other = lax.ppermute(got, "col", swap)
    sent = back_product(core, got, other, own_product(got, turned), turned)
    got = lax.all_to_all(sent, "row", 0, 0)
    item_out = jnp.sum(got[:, :ITEMS].astype(f32), axis=0).astype(bf16)
    grads = lax.all_to_all(last_spread(got), "col", 0, 0)
    half = GRADS // 2
    grad_one = grads[:, :half].astype(f32).reshape(WIDTH, WIDTH)
    grad_two = grads[:, half:].astype(f32).reshape(WIDTH, WIDTH)
    return (item_out, grad_one, grad_two)


def solution(mesh):
    return jax.shard_map(
        shards,
        mesh=mesh,
        in_specs=(
            P(("col", "row"), None),
            P(("col", "row"), None),
            P(),
            P(),
            P("row", "col", None, None, None),
            P("row", "col", None, None),
            P("row", "col"),
        ),
        out_specs=(P(("col", "row"), None), P(), P()),
        check_vma=False,
    )
```

```python
import jax
import jax.numpy as jnp
from jax import lax
from jax.experimental import pallas as pl
from jax.experimental.pallas import tpu as pltpu
from jax.sharding import PartitionSpec as P

TILE = 128
N_ROW = 16
N_COL = 32
SLOTS = 64
BLOCK = 1024
WIDTH = 256
USERS = BLOCK // N_COL
ITEMS = BLOCK // N_ROW
GRADS = 2 * WIDTH // N_COL
PEERS = N_COL // 2
NEAR = 4
RING = (0, 7, 1, 6, 2, 5, 3, 4)
COLS = tuple(2 * y + half for half in range(2) for y in RING)
HALF = BLOCK // 2
VMEM = pl.BlockSpec(memory_space=pltpu.VMEM)
ANY = pl.BlockSpec(memory_space=pl.ANY)
SMEM = pl.BlockSpec(memory_space=pltpu.SMEM)
f32 = jnp.float32
bf16 = jnp.bfloat16


def params(mib=24):
    return pltpu.CompilerParams(vmem_limit_bytes=mib * 1024 * 1024)


def cost(flops, moved):
    return pl.CostEstimate(flops=flops, bytes_accessed=moved, transcendentals=0)


def held(array):
    return pltpu.with_memory_space_constraint(array, pltpu.HBM)


def first_kernel(features, cotangent, out, both, in_sems, out_sems):
    loads = [
        pltpu.make_async_copy(features, both.at[:, :WIDTH], in_sems.at[0]),
        pltpu.make_async_copy(cotangent, both.at[:, WIDTH:], in_sems.at[1]),
    ]
    for copy in loads:
        copy.start()
    for copy in loads:
        copy.wait()
    stores = [pltpu.make_async_copy(both, out.at[i], out_sems.at[i]) for i in range(NEAR)]
    for copy in stores:
        copy.start()
    for copy in stores:
        copy.wait()


def first_spread(features, cotangent):
    return pl.pallas_call(
        first_kernel,
        out_shape=jax.ShapeDtypeStruct((NEAR, ITEMS, 2 * WIDTH), bf16),
        in_specs=[ANY, ANY],
        out_specs=ANY,
        scratch_shapes=[
            pltpu.VMEM((ITEMS, 2 * WIDTH), bf16),
            pltpu.SemaphoreType.DMA((2,)),
            pltpu.SemaphoreType.DMA((NEAR,)),
        ],
        compiler_params=params(),
        cost_estimate=cost(0, 2 * NEAR * ITEMS * 4 * WIDTH),
        name="first_spread",
    )(held(features), held(cotangent))


def second_kernel(rows, after, out):
    for i in range(NEAR):
        out[i] = rows[...]


def second_spread(rows, after):
    return pl.pallas_call(
        second_kernel,
        out_shape=jax.ShapeDtypeStruct((NEAR,) + rows.shape, bf16),
        in_specs=[VMEM, ANY],
        out_specs=VMEM,
        compiler_params=params(),
        name="second_spread",
    )(rows, after)


LOADS = 8
LOAD = SLOTS // LOADS


def dense_kernel(core, count, ids_hbm, tiles, dense, fetched, ids, sems, ids_sem):
    mine = core[0, 0]
    ids_copy = pltpu.make_async_copy(ids_hbm, ids, ids_sem)
    ids_copy.start()
    copies = []
    for i in range(LOADS):
        part = pl.ds(i * LOAD, LOAD)
        copies.append(pltpu.make_async_copy(tiles.at[part], fetched.at[part], sems.at[i]))
    for copy in copies:
        copy.start()
    ids_copy.wait()
    for i in range(LOADS):
        copies[i].wait()
        for k in range(i * LOAD, (i + 1) * LOAD):
            r = ids[0, k]
            c = pl.multiple_of(ids[1, k] * TILE, TILE)
            tile = jnp.where(k < count[0, 0], fetched[k], jnp.zeros((TILE, TILE), bf16))
            place = jnp.where(r < NEAR, 2 * r, 15 - 2 * r)
            for part in range(TILE // USERS):
                half = lax.rem(part + mine, 2)
                row = pl.multiple_of((place + part // 2 * (PEERS // 2)) * USERS, USERS)
                dense[half, pl.ds(row, USERS), pl.ds(c, TILE)] = tile[part * USERS : (part + 1) * USERS]


def make_dense(core, ids, count, tiles):
    return pl.pallas_call(
        dense_kernel,
        out_shape=jax.ShapeDtypeStruct((2, HALF, BLOCK), bf16),
        in_specs=[SMEM, SMEM, ANY, ANY],
        out_specs=VMEM,
        scratch_shapes=[
            pltpu.VMEM((SLOTS, TILE, TILE), bf16),
            pltpu.SMEM((2, SLOTS), jnp.int32),
            pltpu.SemaphoreType.DMA((LOADS,)),
            pltpu.SemaphoreType.DMA,
        ],
        compiler_params=params(),
        cost_estimate=cost(0, 3 * 2 * BLOCK * BLOCK),
        name="dense_block",
    )(core, count, held(ids), held(tiles))


def turn_kernel(dense, after, turned):
    for half in range(2):
        for i in range(0, HALF, TILE):
            for j in range(0, BLOCK, TILE):
                turned[j : j + TILE, half * HALF + i : half * HALF + i + TILE] = dense[half, i : i + TILE, j : j + TILE].T


def turn(dense, after):
    return pl.pallas_call(
        turn_kernel,
        out_shape=jax.ShapeDtypeStruct((BLOCK, BLOCK), bf16),
        in_specs=[VMEM, ANY],
        out_specs=VMEM,
        compiler_params=params(),
        cost_estimate=cost(0, 4 * BLOCK * BLOCK),
        name="turned_block",
    )(dense, after)


CHUNK = 256


def theirs_kernel(dense, items, out):
    for i in range(0, HALF, CHUNK):
        out[i : i + CHUNK] = jnp.dot(dense[1, i : i + CHUNK], items[...], preferred_element_type=f32).astype(bf16)


def mine_kernel(dense, items, out):
    for i in range(0, HALF, CHUNK):
        out[i : i + CHUNK] = jnp.dot(dense[0, i : i + CHUNK], items[...], preferred_element_type=f32)


def add_kernel(mine, other, after, out):
    out[...] = (mine[...] + other[...].astype(f32)).astype(bf16)


def half_product(kernel, dtype, *operands):
    return pl.pallas_call(
        kernel,
        out_shape=jax.ShapeDtypeStruct((HALF, 2 * WIDTH), dtype),
        in_specs=([VMEM, VMEM, ANY])[: len(operands)],
        out_specs=VMEM,
        compiler_params=params(),
        cost_estimate=cost(2 * HALF * BLOCK * 2 * WIDTH, 3 * 1024 * 1024),
        name="user_product",
    )(*operands)


def middle_kernel(parts, out):
    total = parts[0].astype(f32)
    for i in range(1, PEERS):
        total = total + parts[i].astype(f32)
    total = total.astype(bf16)
    for i in range(PEERS):
        out[i] = total


def middle(parts):
    return pl.pallas_call(
        middle_kernel,
        out_shape=jax.ShapeDtypeStruct((PEERS, USERS, 2 * WIDTH), bf16),
        in_specs=[VMEM],
        out_specs=VMEM,
        compiler_params=params(),
        name="middle",
    )(parts)


def layer(core, rows, w1, w2, first, mapped):
    sums = first[:, :WIDTH]
    d_users = first[:, WIDTH:]
    z = jnp.dot(sums, w1, preferred_element_type=f32)
    s = jax.nn.sigmoid(z)
    hidden = (z * s).astype(bf16)
    mapped[rows] = jnp.dot(hidden, w2, preferred_element_type=f32).astype(bf16)
    back = lax.dot_general(d_users, w2, (((1,), (1,)), ((), ())), preferred_element_type=f32)
    d_pre = (back * s * (1.0 + z * (1.0 - s))).astype(bf16)
    is_first = core == 0
    left = jnp.where(is_first, sums, hidden)
    right = jnp.where(is_first, d_pre, d_users)
    return lax.dot_general(left, right, (((0,), (0,)), ((), ())), preferred_element_type=f32)


def block_layer(core, got, w_first, w_second, mapped):
    w1 = w_first[...]
    w2 = w_second[...]
    grads = None
    step = CHUNK // USERS
    for i in range(0, PEERS, step):
        chunk = got[i : i + step].reshape(CHUNK, 2 * WIDTH)
        part = layer(core, slice(i * USERS, i * USERS + CHUNK), w1, w2, chunk, mapped)
        grads = part if grads is None else grads + part
    return grads


def own_kernel(core, got, w_first, w_second, turned, out, grads, mapped):
    grads[...] = block_layer(core[0, 0], got, w_first, w_second, mapped)
    for i in range(0, BLOCK, CHUNK):
        out[i : i + CHUNK] = jnp.dot(turned[i : i + CHUNK, :HALF], mapped[...], preferred_element_type=f32)


def own_product(core, got, w_first, w_second, turned):
    return pl.pallas_call(
        own_kernel,
        out_shape=(jax.ShapeDtypeStruct((BLOCK, WIDTH), f32), jax.ShapeDtypeStruct((WIDTH, WIDTH), f32)),
        in_specs=[SMEM, VMEM, VMEM, VMEM, VMEM],
        out_specs=(VMEM, VMEM),
        scratch_shapes=[pltpu.VMEM((HALF, WIDTH), bf16)],
        compiler_params=params(),
        cost_estimate=cost(2 * BLOCK * HALF * WIDTH, 3 * 1024 * 1024),
        name="own_product",
    )(core, got, w_first, w_second, turned)


def back_kernel(core, got, w_first, w_second, own, own_grads, turned, out, mapped):
    grads = own_grads[...] + block_layer(core[0, 0], got, w_first, w_second, mapped)
    grads = grads.astype(bf16)
    for i in range(NEAR):
        rows = slice(i * CHUNK, (i + 1) * CHUNK)
        part = own[rows] + jnp.dot(turned[rows, HALF:], mapped[...], preferred_element_type=f32)
        out[i, :CHUNK] = part.astype(bf16)
        out[i, CHUNK:] = grads[i * ITEMS : (i + 1) * ITEMS]


def back_product(core, got, w_first, w_second, own, own_grads, turned):
    return pl.pallas_call(
        back_kernel,
        out_shape=jax.ShapeDtypeStruct((NEAR, CHUNK + ITEMS, WIDTH), bf16),
        in_specs=[SMEM, VMEM, VMEM, VMEM, VMEM, VMEM, VMEM],
        out_specs=VMEM,
        scratch_shapes=[pltpu.VMEM((HALF, WIDTH), bf16)],
        compiler_params=params(),
        name="back_product",
    )(core, got, w_first, w_second, own, own_grads, turned)


def sum_kernel(got, out):
    total = got[0].astype(f32)
    for i in range(1, NEAR):
        total = total + got[i].astype(f32)
    total = total.astype(bf16)
    for i in range(NEAR):
        out[i, :ITEMS] = total[i * ITEMS : (i + 1) * ITEMS]
        out[i, ITEMS:] = total[CHUNK:]


def sum_sides(got):
    return pl.pallas_call(
        sum_kernel,
        out_shape=jax.ShapeDtypeStruct((NEAR, 2 * ITEMS, WIDTH), bf16),
        in_specs=[VMEM],
        out_specs=VMEM,
        compiler_params=params(),
        name="sum_sides",
    )(got)


def last_kernel(got, item_out, out):
    total = got[0].astype(f32)
    for i in range(1, NEAR):
        total = total + got[i].astype(f32)
    total = total.astype(bf16)
    item_out[...] = total[:ITEMS]
    for i in range(2 * NEAR):
        out[i] = total[ITEMS:]


def last_spread(got):
    return pl.pallas_call(
        last_kernel,
        out_shape=(
            jax.ShapeDtypeStruct((ITEMS, WIDTH), bf16),
            jax.ShapeDtypeStruct((2 * NEAR, ITEMS, WIDTH), bf16),
        ),
        in_specs=[VMEM],
        out_specs=(VMEM, VMEM),
        compiler_params=params(),
        name="last_spread",
    )(got)


def shards(features, cotangent, w_first, w_second, adjacency_tiles, tile_ids, counts):
    core = lax.rem(lax.axis_index("col"), 2).reshape(1, 1)
    same_core = [[2 * i + k for i in COLS] for k in range(2)]
    same_x = [[NEAR * i + k for k in range(NEAR)] for i in range(NEAR)]
    same_z = [[NEAR * i + k for i in range(NEAR)] for k in range(NEAR)]
    sides = [
        [(NEAR * i + k) * N_COL + 2 * q + h for h in range(2) for i in range(NEAR)]
        for k in range(NEAR)
        for q in range(PEERS)
    ]
    swap = [(i, i ^ 1) for i in range(N_COL)]
    spread = first_spread(features, cotangent)
    dense = make_dense(core, tile_ids[0, 0], counts, adjacency_tiles[0, 0])
    items = lax.all_to_all(spread, "row", 0, 0, axis_index_groups=same_x).reshape(NEAR * ITEMS, 2 * WIDTH)
    items = lax.all_to_all(second_spread(items, dense), "row", 0, 0, axis_index_groups=same_z)
    items = items.reshape(BLOCK, 2 * WIDTH)
    theirs = half_product(theirs_kernel, bf16, dense, items)
    other = lax.ppermute(theirs, "col", swap)
    mine = half_product(mine_kernel, f32, dense, items)
    turned = turn(dense, theirs)
    sums = half_product(add_kernel, bf16, mine, other, turned).reshape(PEERS, USERS, 2 * WIDTH)
    parts = lax.all_to_all(sums, "col", 0, 0, axis_index_groups=same_core)
    got = lax.all_to_all(middle(parts), "col", 0, 0, axis_index_groups=same_core)
    other = lax.ppermute(got, "col", swap)
    own, own_grads = own_product(core, got, w_first, w_second, turned)
    sent = back_product(core, other, w_first, w_second, own, own_grads, turned)
    sent = sum_sides(lax.all_to_all(sent, "row", 0, 0, axis_index_groups=same_z))
    item_out, grads = last_spread(lax.all_to_all(sent, "row", 0, 0, axis_index_groups=same_x))
    grads = lax.all_to_all(grads, ("row", "col"), 0, 0, axis_index_groups=sides).astype(f32)
    grad_one = grads[:NEAR].reshape(WIDTH, WIDTH)
    grad_two = grads[NEAR:].reshape(WIDTH, WIDTH)
    return (item_out, grad_one, grad_two)


def solution(mesh):
    return jax.shard_map(
        shards,
        mesh=mesh,
        in_specs=(
            P(("col", "row"), None),
            P(("col", "row"), None),
            P(),
            P(),
            P("row", "col", None, None, None),
            P("row", "col", None, None),
            P("row", "col"),
        ),
        out_specs=(P(("col", "row"), None), P(), P()),
        check_vma=False,
    )
```

```python
import jax
import jax.numpy as jnp
from jax import lax
from jax.experimental import pallas as pl
from jax.experimental.pallas import tpu as pltpu
from jax.sharding import PartitionSpec as P

TILE = 128
N_ROW = 16
N_COL = 32
SLOTS = 64
BLOCK = 1024
WIDTH = 256
USERS = BLOCK // N_COL
ITEMS = BLOCK // N_ROW
GRADS = 2 * WIDTH // N_COL
PEERS = N_COL // 2
NEAR = 4
SIDES = (0, 2, 1, 3)
RING = (0, 7, 1, 6, 2, 5, 3, 4)
COLS = tuple(2 * y + half for half in range(2) for y in RING)
HALF = BLOCK // 2
VMEM = pl.BlockSpec(memory_space=pltpu.VMEM)
ANY = pl.BlockSpec(memory_space=pl.ANY)
SMEM = pl.BlockSpec(memory_space=pltpu.SMEM)
f32 = jnp.float32
bf16 = jnp.bfloat16


def params(mib=24):
    return pltpu.CompilerParams(vmem_limit_bytes=mib * 1024 * 1024)


def cost(flops, moved):
    return pl.CostEstimate(flops=flops, bytes_accessed=moved, transcendentals=0)


def held(array):
    return pltpu.with_memory_space_constraint(array, pltpu.HBM)


def first_kernel(features, cotangent, out, both, in_sems, out_sems):
    loads = [
        pltpu.make_async_copy(features, both.at[:, :WIDTH], in_sems.at[0]),
        pltpu.make_async_copy(cotangent, both.at[:, WIDTH:], in_sems.at[1]),
    ]
    for copy in loads:
        copy.start()
    for copy in loads:
        copy.wait()
    stores = [pltpu.make_async_copy(both, out.at[i], out_sems.at[i]) for i in range(NEAR)]
    for copy in stores:
        copy.start()
    for copy in stores:
        copy.wait()


def first_spread(features, cotangent):
    return pl.pallas_call(
        first_kernel,
        out_shape=jax.ShapeDtypeStruct((NEAR, ITEMS, 2 * WIDTH), bf16),
        in_specs=[ANY, ANY],
        out_specs=ANY,
        scratch_shapes=[
            pltpu.VMEM((ITEMS, 2 * WIDTH), bf16),
            pltpu.SemaphoreType.DMA((2,)),
            pltpu.SemaphoreType.DMA((NEAR,)),
        ],
        compiler_params=params(),
        cost_estimate=cost(0, 2 * NEAR * ITEMS * 4 * WIDTH),
        name="first_spread",
    )(held(features), held(cotangent))


def second_kernel(rows, after, out):
    for i in range(NEAR):
        out[i] = rows[...]


def second_spread(rows, after):
    return pl.pallas_call(
        second_kernel,
        out_shape=jax.ShapeDtypeStruct((NEAR,) + rows.shape, bf16),
        in_specs=[VMEM, ANY],
        out_specs=VMEM,
        compiler_params=params(),
        name="second_spread",
    )(rows, after)


LOADS = 8
LOAD = SLOTS // LOADS


def dense_kernel(core, count, ids_hbm, tiles, dense, fetched, ids, sems, ids_sem):
    mine = core[0, 0]
    ids_copy = pltpu.make_async_copy(ids_hbm, ids, ids_sem)
    ids_copy.start()
    copies = []
    for i in range(LOADS):
        part = pl.ds(i * LOAD, LOAD)
        copies.append(pltpu.make_async_copy(tiles.at[part], fetched.at[part], sems.at[i]))
    for copy in copies:
        copy.start()
    ids_copy.wait()
    for i in range(LOADS):
        copies[i].wait()
        for k in range(i * LOAD, (i + 1) * LOAD):
            r = ids[0, k]
            c = ids[1, k]
            side = lax.rem(c // 2, 2) * 2 + c // 4
            c = pl.multiple_of((2 * side + lax.rem(c, 2)) * TILE, TILE)
            tile = jnp.where(k < count[0, 0], fetched[k], jnp.zeros((TILE, TILE), bf16))
            place = jnp.where(r < NEAR, 2 * r, 15 - 2 * r)
            for part in range(TILE // USERS):
                half = lax.rem(part + mine, 2)
                row = pl.multiple_of((place + part // 2 * (PEERS // 2)) * USERS, USERS)
                dense[half, pl.ds(row, USERS), pl.ds(c, TILE)] = tile[part * USERS : (part + 1) * USERS]


def make_dense(core, ids, count, tiles):
    return pl.pallas_call(
        dense_kernel,
        out_shape=jax.ShapeDtypeStruct((2, HALF, BLOCK), bf16),
        in_specs=[SMEM, SMEM, ANY, ANY],
        out_specs=VMEM,
        scratch_shapes=[
            pltpu.VMEM((SLOTS, TILE, TILE), bf16),
            pltpu.SMEM((2, SLOTS), jnp.int32),
            pltpu.SemaphoreType.DMA((LOADS,)),
            pltpu.SemaphoreType.DMA,
        ],
        compiler_params=params(),
        cost_estimate=cost(0, 3 * 2 * BLOCK * BLOCK),
        name="dense_block",
    )(core, count, held(ids), held(tiles))


def turn_kernel(dense, after, turned):
    for half in range(2):
        for i in range(0, HALF, TILE):
            for j in range(0, BLOCK, TILE):
                turned[j : j + TILE, half * HALF + i : half * HALF + i + TILE] = dense[half, i : i + TILE, j : j + TILE].T


def turn(dense, after):
    return pl.pallas_call(
        turn_kernel,
        out_shape=jax.ShapeDtypeStruct((BLOCK, BLOCK), bf16),
        in_specs=[VMEM, ANY],
        out_specs=VMEM,
        compiler_params=params(),
        cost_estimate=cost(0, 4 * BLOCK * BLOCK),
        name="turned_block",
    )(dense, after)


CHUNK = 256


def theirs_kernel(dense, items, out):
    for i in range(0, HALF, CHUNK):
        out[i : i + CHUNK] = jnp.dot(dense[1, i : i + CHUNK], items[...], preferred_element_type=f32).astype(bf16)


def mine_kernel(dense, items, out):
    for i in range(0, HALF, CHUNK):
        out[i : i + CHUNK] = jnp.dot(dense[0, i : i + CHUNK], items[...], preferred_element_type=f32)


def add_kernel(mine, other, after, out):
    out[...] = (mine[...] + other[...].astype(f32)).astype(bf16)


def half_product(kernel, dtype, *operands):
    return pl.pallas_call(
        kernel,
        out_shape=jax.ShapeDtypeStruct((HALF, 2 * WIDTH), dtype),
        in_specs=([VMEM, VMEM, ANY])[: len(operands)],
        out_specs=VMEM,
        compiler_params=params(),
        cost_estimate=cost(2 * HALF * BLOCK * 2 * WIDTH, 3 * 1024 * 1024),
        name="user_product",
    )(*operands)


def middle_kernel(parts, out):
    total = parts[0].astype(f32)
    for i in range(1, PEERS):
        total = total + parts[i].astype(f32)
    total = total.astype(bf16)
    for i in range(PEERS):
        out[i] = total


def middle(parts):
    return pl.pallas_call(
        middle_kernel,
        out_shape=jax.ShapeDtypeStruct((PEERS, USERS, 2 * WIDTH), bf16),
        in_specs=[VMEM],
        out_specs=VMEM,
        compiler_params=params(),
        name="middle",
    )(parts)


def layer(core, rows, w1, w2, first, mapped):
    sums = first[:, :WIDTH]
    d_users = first[:, WIDTH:]
    z = jnp.dot(sums, w1, preferred_element_type=f32)
    s = jax.nn.sigmoid(z)
    hidden = (z * s).astype(bf16)
    mapped[rows] = jnp.dot(hidden, w2, preferred_element_type=f32).astype(bf16)
    back = lax.dot_general(d_users, w2, (((1,), (1,)), ((), ())), preferred_element_type=f32)
    d_pre = (back * s * (1.0 + z * (1.0 - s))).astype(bf16)
    is_first = core == 0
    left = jnp.where(is_first, sums, hidden)
    right = jnp.where(is_first, d_pre, d_users)
    return lax.dot_general(left, right, (((0,), (0,)), ((), ())), preferred_element_type=f32)


def block_layer(core, got, w_first, w_second, mapped):
    w1 = w_first[...]
    w2 = w_second[...]
    grads = None
    step = CHUNK // USERS
    for i in range(0, PEERS, step):
        chunk = got[i : i + step].reshape(CHUNK, 2 * WIDTH)
        part = layer(core, slice(i * USERS, i * USERS + CHUNK), w1, w2, chunk, mapped)
        grads = part if grads is None else grads + part
    return grads


def own_kernel(core, got, w_first, w_second, turned, out, grads, mapped):
    grads[...] = block_layer(core[0, 0], got, w_first, w_second, mapped)
    for i in range(0, BLOCK, CHUNK):
        out[i : i + CHUNK] = jnp.dot(turned[i : i + CHUNK, :HALF], mapped[...], preferred_element_type=f32)


def own_product(core, got, w_first, w_second, turned):
    return pl.pallas_call(
        own_kernel,
        out_shape=(jax.ShapeDtypeStruct((BLOCK, WIDTH), f32), jax.ShapeDtypeStruct((WIDTH, WIDTH), f32)),
        in_specs=[SMEM, VMEM, VMEM, VMEM, VMEM],
        out_specs=(VMEM, VMEM),
        scratch_shapes=[pltpu.VMEM((HALF, WIDTH), bf16)],
        compiler_params=params(),
        cost_estimate=cost(2 * BLOCK * HALF * WIDTH, 3 * 1024 * 1024),
        name="own_product",
    )(core, got, w_first, w_second, turned)


def back_kernel(core, got, w_first, w_second, own, own_grads, turned, out, mapped):
    grads = own_grads[...] + block_layer(core[0, 0], got, w_first, w_second, mapped)
    grads = grads.astype(bf16)
    for i in range(NEAR):
        rows = slice(i * CHUNK, (i + 1) * CHUNK)
        part = own[rows] + jnp.dot(turned[rows, HALF:], mapped[...], preferred_element_type=f32)
        out[i, :CHUNK] = part.astype(bf16)
        out[i, CHUNK:] = grads[SIDES[i] * ITEMS : (SIDES[i] + 1) * ITEMS]


def back_product(core, got, w_first, w_second, own, own_grads, turned):
    return pl.pallas_call(
        back_kernel,
        out_shape=jax.ShapeDtypeStruct((NEAR, CHUNK + ITEMS, WIDTH), bf16),
        in_specs=[SMEM, VMEM, VMEM, VMEM, VMEM, VMEM, VMEM],
        out_specs=VMEM,
        scratch_shapes=[pltpu.VMEM((HALF, WIDTH), bf16)],
        compiler_params=params(),
        name="back_product",
    )(core, got, w_first, w_second, own, own_grads, turned)


def sum_kernel(got, out):
    total = got[0].astype(f32)
    for i in range(1, NEAR):
        total = total + got[i].astype(f32)
    total = total.astype(bf16)
    for i in range(NEAR):
        out[i, :ITEMS] = total[i * ITEMS : (i + 1) * ITEMS]
        out[i, ITEMS:] = total[CHUNK:]


def sum_sides(got):
    return pl.pallas_call(
        sum_kernel,
        out_shape=jax.ShapeDtypeStruct((NEAR, 2 * ITEMS, WIDTH), bf16),
        in_specs=[VMEM],
        out_specs=VMEM,
        compiler_params=params(),
        name="sum_sides",
    )(got)


def spread_kernel(got, out):
    total = got[0, ITEMS:].astype(f32)
    for i in range(1, NEAR):
        total = total + got[i, ITEMS:].astype(f32)
    total = total.astype(bf16)
    for i in range(2 * NEAR):
        out[i] = total


def last_spread(got):
    return pl.pallas_call(
        spread_kernel,
        out_shape=jax.ShapeDtypeStruct((2 * NEAR, ITEMS, WIDTH), bf16),
        in_specs=[VMEM],
        out_specs=VMEM,
        compiler_params=params(),
        name="last_spread",
    )(got)


def finish_kernel(got, grads, item_out, grad_one, grad_two, items, both, sems):
    copies = [
        pltpu.make_async_copy(items, item_out, sems.at[0]),
        pltpu.make_async_copy(both.at[0], grad_one, sems.at[1]),
        pltpu.make_async_copy(both.at[1], grad_two, sems.at[2]),
    ]
    for half in range(2):
        for i in range(NEAR):
            both[half, i * ITEMS : (i + 1) * ITEMS] = grads[half * NEAR + i].astype(f32)
        copies[1 + half].start()
    total = got[0, :ITEMS].astype(f32)
    for i in range(1, NEAR):
        total = total + got[i, :ITEMS].astype(f32)
    items[...] = total.astype(bf16)
    copies[0].start()
    for copy in copies:
        copy.wait()


def finish(got, grads):
    square = jax.ShapeDtypeStruct((WIDTH, WIDTH), f32)
    return pl.pallas_call(
        finish_kernel,
        out_shape=(jax.ShapeDtypeStruct((ITEMS, WIDTH), bf16), square, square),
        in_specs=[VMEM, VMEM],
        out_specs=(ANY, ANY, ANY),
        scratch_shapes=[
            pltpu.VMEM((ITEMS, WIDTH), bf16),
            pltpu.VMEM((2, WIDTH, WIDTH), f32),
            pltpu.SemaphoreType.DMA((3,)),
        ],
        compiler_params=params(),
        name="finish",
    )(got, grads)


def shards(features, cotangent, w_first, w_second, adjacency_tiles, tile_ids, counts):
    core = lax.rem(lax.axis_index("col"), 2).reshape(1, 1)
    same_core = [[2 * i + k for i in COLS] for k in range(2)]
    same_x = [[NEAR * i + k for k in range(NEAR)] for i in range(NEAR)]
    same_z = [[NEAR * i + k for i in SIDES] for k in range(NEAR)]
    sides = [
        [(NEAR * i + k) * N_COL + 2 * q + h for h in range(2) for i in range(NEAR)]
        for k in range(NEAR)
        for q in range(PEERS)
    ]
    swap = [(i, i ^ 1) for i in range(N_COL)]
    spread = first_spread(features, cotangent)
    dense = make_dense(core, tile_ids[0, 0], counts, adjacency_tiles[0, 0])
    items = lax.all_to_all(spread, "row", 0, 0, axis_index_groups=same_x).reshape(NEAR * ITEMS, 2 * WIDTH)
    items = lax.all_to_all(second_spread(items, dense), "row", 0, 0, axis_index_groups=same_z)
    items = items.reshape(BLOCK, 2 * WIDTH)
    theirs = half_product(theirs_kernel, bf16, dense, items)
    other = lax.ppermute(theirs, "col", swap)
    mine = half_product(mine_kernel, f32, dense, items)
    turned = turn(dense, theirs)
    sums = half_product(add_kernel, bf16, mine, other, turned).reshape(PEERS, USERS, 2 * WIDTH)
    parts = lax.all_to_all(sums, "col", 0, 0, axis_index_groups=same_core)
    got = lax.all_to_all(middle(parts), "col", 0, 0, axis_index_groups=same_core)
    other = lax.ppermute(got, "col", swap)
    own, own_grads = own_product(core, got, w_first, w_second, turned)
    sent = back_product(core, other, w_first, w_second, own, own_grads, turned)
    sent = sum_sides(lax.all_to_all(sent, "row", 0, 0, axis_index_groups=same_z))
    got = lax.all_to_all(sent, "row", 0, 0, axis_index_groups=same_x)
    grads = lax.all_to_all(last_spread(got), ("row", "col"), 0, 0, axis_index_groups=sides)
    return finish(got, grads)


def solution(mesh):
    return jax.shard_map(
        shards,
        mesh=mesh,
        in_specs=(
            P(("col", "row"), None),
            P(("col", "row"), None),
            P(),
            P(),
            P("row", "col", None, None, None),
            P("row", "col", None, None),
            P("row", "col"),
        ),
        out_specs=(P(("col", "row"), None), P(), P()),
        check_vma=False,
    )
```

```python
import jax
import jax.numpy as jnp
from jax import lax
from jax.experimental import pallas as pl
from jax.experimental.pallas import tpu as pltpu
from jax.sharding import PartitionSpec as P

TILE = 128
N_ROW = 16
N_COL = 32
SLOTS = 64
BLOCK = 1024
WIDTH = 256
USERS = BLOCK // N_COL
ITEMS = BLOCK // N_ROW
GRADS = 2 * WIDTH // N_COL
PEERS = N_COL // 2
NEAR = 4
SIDES = (0, 2, 1, 3)
RING = (0, 7, 1, 6, 2, 5, 3, 4)
COLS = tuple(2 * y + half for half in range(2) for y in RING)
HALF = BLOCK // 2
VMEM = pl.BlockSpec(memory_space=pltpu.VMEM)
ANY = pl.BlockSpec(memory_space=pl.ANY)
SMEM = pl.BlockSpec(memory_space=pltpu.SMEM)
f32 = jnp.float32
bf16 = jnp.bfloat16


def params(mib=24):
    return pltpu.CompilerParams(vmem_limit_bytes=mib * 1024 * 1024)


def cost(flops, moved):
    return pl.CostEstimate(flops=flops, bytes_accessed=moved, transcendentals=0)


def held(array):
    return pltpu.with_memory_space_constraint(array, pltpu.HBM)


def first_kernel(features, cotangent, out, both, in_sems, out_sems):
    loads = [
        pltpu.make_async_copy(features, both.at[:, :WIDTH], in_sems.at[0]),
        pltpu.make_async_copy(cotangent, both.at[:, WIDTH:], in_sems.at[1]),
    ]
    for copy in loads:
        copy.start()
    for copy in loads:
        copy.wait()
    stores = [pltpu.make_async_copy(both, out.at[i], out_sems.at[i]) for i in range(NEAR)]
    for copy in stores:
        copy.start()
    for copy in stores:
        copy.wait()


def first_spread(features, cotangent):
    return pl.pallas_call(
        first_kernel,
        out_shape=jax.ShapeDtypeStruct((NEAR, ITEMS, 2 * WIDTH), bf16),
        in_specs=[ANY, ANY],
        out_specs=ANY,
        scratch_shapes=[
            pltpu.VMEM((ITEMS, 2 * WIDTH), bf16),
            pltpu.SemaphoreType.DMA((2,)),
            pltpu.SemaphoreType.DMA((NEAR,)),
        ],
        compiler_params=params(),
        cost_estimate=cost(0, 2 * NEAR * ITEMS * 4 * WIDTH),
        name="first_spread",
    )(held(features), held(cotangent))


def second_kernel(rows, after, out):
    for i in range(NEAR):
        out[i] = rows[...]


def second_spread(rows, after):
    return pl.pallas_call(
        second_kernel,
        out_shape=jax.ShapeDtypeStruct((NEAR,) + rows.shape, bf16),
        in_specs=[VMEM, ANY],
        out_specs=VMEM,
        compiler_params=params(),
        name="second_spread",
    )(rows, after)


LOADS = 8
LOAD = SLOTS // LOADS


def dense_kernel(core, count, ids_hbm, tiles, dense, fetched, ids, sems, ids_sem):
    mine = core[0, 0]
    ids_copy = pltpu.make_async_copy(ids_hbm, ids, ids_sem)
    ids_copy.start()
    copies = []
    for i in range(LOADS):
        part = pl.ds(i * LOAD, LOAD)
        copies.append(pltpu.make_async_copy(tiles.at[part], fetched.at[part], sems.at[i]))
    for copy in copies:
        copy.start()
    ids_copy.wait()
    for i in range(LOADS):
        copies[i].wait()
        for k in range(i * LOAD, (i + 1) * LOAD):
            r = ids[0, k]
            c = ids[1, k]
            side = lax.rem(c // 2, 2) * 2 + c // 4
            c = pl.multiple_of((2 * side + lax.rem(c, 2)) * TILE, TILE)
            tile = jnp.where(k < count[0, 0], fetched[k], jnp.zeros((TILE, TILE), bf16))
            place = jnp.where(r < NEAR, 2 * r, 15 - 2 * r)
            for part in range(TILE // USERS):
                half = lax.rem(part + mine, 2)
                row = pl.multiple_of((place + part // 2 * (PEERS // 2)) * USERS, USERS)
                dense[half, pl.ds(row, USERS), pl.ds(c, TILE)] = tile[part * USERS : (part + 1) * USERS]


def make_dense(core, ids, count, tiles):
    return pl.pallas_call(
        dense_kernel,
        out_shape=jax.ShapeDtypeStruct((2, HALF, BLOCK), bf16),
        in_specs=[SMEM, SMEM, ANY, ANY],
        out_specs=VMEM,
        scratch_shapes=[
            pltpu.VMEM((SLOTS, TILE, TILE), bf16),
            pltpu.SMEM((2, SLOTS), jnp.int32),
            pltpu.SemaphoreType.DMA((LOADS,)),
            pltpu.SemaphoreType.DMA,
        ],
        compiler_params=params(),
        cost_estimate=cost(0, 3 * 2 * BLOCK * BLOCK),
        name="dense_block",
    )(core, count, held(ids), held(tiles))


def turn_kernel(dense, after, turned):
    for half in range(2):
        for i in range(0, HALF, TILE):
            for j in range(0, BLOCK, TILE):
                turned[j : j + TILE, half * HALF + i : half * HALF + i + TILE] = dense[half, i : i + TILE, j : j + TILE].T


def turn(dense, after):
    return pl.pallas_call(
        turn_kernel,
        out_shape=jax.ShapeDtypeStruct((BLOCK, BLOCK), bf16),
        in_specs=[VMEM, ANY],
        out_specs=VMEM,
        compiler_params=params(),
        cost_estimate=cost(0, 4 * BLOCK * BLOCK),
        name="turned_block",
    )(dense, after)


CHUNK = 256


def theirs_kernel(dense, items, out):
    for i in range(0, HALF, CHUNK):
        out[i : i + CHUNK] = jnp.dot(dense[1, i : i + CHUNK], items[...], preferred_element_type=f32).astype(bf16)


def mine_kernel(dense, items, out):
    for i in range(0, HALF, CHUNK):
        out[i : i + CHUNK] = jnp.dot(dense[0, i : i + CHUNK], items[...], preferred_element_type=f32)


def add_kernel(mine, other, after, out):
    out[...] = (mine[...] + other[...].astype(f32)).astype(bf16)


def half_product(kernel, dtype, *operands):
    return pl.pallas_call(
        kernel,
        out_shape=jax.ShapeDtypeStruct((HALF, 2 * WIDTH), dtype),
        in_specs=([VMEM, VMEM, ANY])[: len(operands)],
        out_specs=VMEM,
        compiler_params=params(),
        cost_estimate=cost(2 * HALF * BLOCK * 2 * WIDTH, 3 * 1024 * 1024),
        name="user_product",
    )(*operands)


def middle_kernel(parts, out):
    total = parts[0].astype(f32)
    for i in range(1, PEERS):
        total = total + parts[i].astype(f32)
    total = total.astype(bf16)
    for i in range(PEERS):
        out[i] = total


def middle(parts):
    return pl.pallas_call(
        middle_kernel,
        out_shape=jax.ShapeDtypeStruct((PEERS, USERS, 2 * WIDTH), bf16),
        in_specs=[VMEM],
        out_specs=VMEM,
        compiler_params=params(),
        name="middle",
    )(parts)


def layer_kernel(core, got, w_first, w_second, sent, kept):
    w1 = w_first[...]
    w2 = w_second[...]
    over_users = (((0,), (0,)), ((), ()))
    grad_one = jnp.zeros((WIDTH, WIDTH), f32)
    grad_two = jnp.zeros((WIDTH, WIDTH), f32)
    step = CHUNK // USERS
    for i in range(0, PEERS, step):
        chunk = got[i : i + step].reshape(CHUNK, 2 * WIDTH)
        sums = chunk[:, :WIDTH]
        d_users = chunk[:, WIDTH:]
        z = jnp.dot(sums, w1, preferred_element_type=f32)
        s = jax.nn.sigmoid(z)
        hidden = (z * s).astype(bf16)
        rows = slice(i * USERS, i * USERS + CHUNK)
        sent[rows] = jnp.dot(hidden, w2, preferred_element_type=f32).astype(bf16)
        back = lax.dot_general(d_users, w2, (((1,), (1,)), ((), ())), preferred_element_type=f32)
        d_pre = (back * s * (1.0 + z * (1.0 - s))).astype(bf16)
        grad_one += lax.dot_general(sums, d_pre, over_users, preferred_element_type=f32)
        grad_two += lax.dot_general(hidden, d_users, over_users, preferred_element_type=f32)
    is_first = core[0, 0] == 0
    kept[...] = jnp.where(is_first, grad_one, grad_two)
    sent[HALF:] = jnp.where(is_first, grad_two, grad_one).astype(bf16)


def layer(core, got, w_first, w_second):
    return pl.pallas_call(
        layer_kernel,
        out_shape=(
            jax.ShapeDtypeStruct((HALF + WIDTH, WIDTH), bf16),
            jax.ShapeDtypeStruct((WIDTH, WIDTH), f32),
        ),
        in_specs=[SMEM, VMEM, VMEM, VMEM],
        out_specs=(VMEM, VMEM),
        compiler_params=params(),
        name="layer",
    )(core, got, w_first, w_second)


def own_kernel(sent, turned, out):
    for i in range(0, BLOCK, CHUNK):
        out[i : i + CHUNK] = jnp.dot(turned[i : i + CHUNK, :HALF], sent[:HALF], preferred_element_type=f32)


def own_product(sent, turned):
    return pl.pallas_call(
        own_kernel,
        out_shape=jax.ShapeDtypeStruct((BLOCK, WIDTH), f32),
        in_specs=[VMEM, VMEM],
        out_specs=VMEM,
        compiler_params=params(),
        cost_estimate=cost(2 * BLOCK * HALF * WIDTH, 3 * 1024 * 1024),
        name="own_product",
    )(sent, turned)


def back_kernel(got, own, kept, turned, out):
    grads = (kept[...] + got[HALF:].astype(f32)).astype(bf16)
    for i in range(NEAR):
        rows = slice(i * CHUNK, (i + 1) * CHUNK)
        part = own[rows] + jnp.dot(turned[rows, HALF:], got[:HALF], preferred_element_type=f32)
        out[i, :CHUNK] = part.astype(bf16)
        out[i, CHUNK:] = grads[SIDES[i] * ITEMS : (SIDES[i] + 1) * ITEMS]


def back_product(got, own, kept, turned):
    return pl.pallas_call(
        back_kernel,
        out_shape=jax.ShapeDtypeStruct((NEAR, CHUNK + ITEMS, WIDTH), bf16),
        in_specs=[VMEM, VMEM, VMEM, VMEM],
        out_specs=VMEM,
        compiler_params=params(),
        name="back_product",
    )(got, own, kept, turned)


def sum_kernel(got, out):
    total = got[0].astype(f32)
    for i in range(1, NEAR):
        total = total + got[i].astype(f32)
    total = total.astype(bf16)
    for i in range(NEAR):
        out[i, :ITEMS] = total[i * ITEMS : (i + 1) * ITEMS]
        out[i, ITEMS:] = total[CHUNK:]


def sum_sides(got):
    return pl.pallas_call(
        sum_kernel,
        out_shape=jax.ShapeDtypeStruct((NEAR, 2 * ITEMS, WIDTH), bf16),
        in_specs=[VMEM],
        out_specs=VMEM,
        compiler_params=params(),
        name="sum_sides",
    )(got)


def spread_kernel(got, out):
    total = got[0, ITEMS:].astype(f32)
    for i in range(1, NEAR):
        total = total + got[i, ITEMS:].astype(f32)
    total = total.astype(bf16)
    for i in range(2 * NEAR):
        out[i] = total


def last_spread(got):
    return pl.pallas_call(
        spread_kernel,
        out_shape=jax.ShapeDtypeStruct((2 * NEAR, ITEMS, WIDTH), bf16),
        in_specs=[VMEM],
        out_specs=VMEM,
        compiler_params=params(),
        name="last_spread",
    )(got)


def finish_kernel(got, grads, item_out, grad_one, grad_two, items, both, sems):
    copies = [
        pltpu.make_async_copy(items, item_out, sems.at[0]),
        pltpu.make_async_copy(both.at[0], grad_one, sems.at[1]),
        pltpu.make_async_copy(both.at[1], grad_two, sems.at[2]),
    ]
    for half in range(2):
        for i in range(NEAR):
            both[half, SIDES[i] * ITEMS : (SIDES[i] + 1) * ITEMS] = grads[2 * i + half].astype(f32)
        copies[1 + half].start()
    total = got[0, :ITEMS].astype(f32)
    for i in range(1, NEAR):
        total = total + got[i, :ITEMS].astype(f32)
    items[...] = total.astype(bf16)
    copies[0].start()
    for copy in copies:
        copy.wait()


def finish(got, grads):
    square = jax.ShapeDtypeStruct((WIDTH, WIDTH), f32)
    return pl.pallas_call(
        finish_kernel,
        out_shape=(jax.ShapeDtypeStruct((ITEMS, WIDTH), bf16), square, square),
        in_specs=[VMEM, VMEM],
        out_specs=(ANY, ANY, ANY),
        scratch_shapes=[
            pltpu.VMEM((ITEMS, WIDTH), bf16),
            pltpu.VMEM((2, WIDTH, WIDTH), f32),
            pltpu.SemaphoreType.DMA((3,)),
        ],
        compiler_params=params(),
        name="finish",
    )(got, grads)


def shards(features, cotangent, w_first, w_second, adjacency_tiles, tile_ids, counts):
    core = lax.rem(lax.axis_index("col"), 2).reshape(1, 1)
    same_core = [[2 * i + k for i in COLS] for k in range(2)]
    same_x = [[NEAR * i + k for k in range(NEAR)] for i in range(NEAR)]
    same_z = [[NEAR * i + k for i in SIDES] for k in range(NEAR)]
    sides = [
        [(NEAR * i + k) * N_COL + 2 * q + h for i in SIDES for h in range(2)]
        for k in range(NEAR)
        for q in range(PEERS)
    ]
    swap = [(i, i ^ 1) for i in range(N_COL)]
    spread = first_spread(features, cotangent)
    dense = make_dense(core, tile_ids[0, 0], counts, adjacency_tiles[0, 0])
    items = lax.all_to_all(spread, "row", 0, 0, axis_index_groups=same_x).reshape(NEAR * ITEMS, 2 * WIDTH)
    items = lax.all_to_all(second_spread(items, dense), "row", 0, 0, axis_index_groups=same_z)
    items = items.reshape(BLOCK, 2 * WIDTH)
    theirs = half_product(theirs_kernel, bf16, dense, items)
    other = lax.ppermute(theirs, "col", swap)
    mine = half_product(mine_kernel, f32, dense, items)
    turned = turn(dense, theirs)
    sums = half_product(add_kernel, bf16, mine, other, turned).reshape(PEERS, USERS, 2 * WIDTH)
    parts = lax.all_to_all(sums, "col", 0, 0, axis_index_groups=same_core)
    got = lax.all_to_all(middle(parts), "col", 0, 0, axis_index_groups=same_core)
    mapped, kept = layer(core, got, w_first, w_second)
    other = lax.ppermute(mapped, "col", swap)
    sent = back_product(other, own_product(mapped, turned), kept, turned)
    sent = sum_sides(lax.all_to_all(sent, "row", 0, 0, axis_index_groups=same_z))
    got = lax.all_to_all(sent, "row", 0, 0, axis_index_groups=same_x)
    grads = lax.all_to_all(last_spread(got), ("row", "col"), 0, 0, axis_index_groups=sides)
    return finish(got, grads)


def solution(mesh):
    return jax.shard_map(
        shards,
        mesh=mesh,
        in_specs=(
            P(("col", "row"), None),
            P(("col", "row"), None),
            P(),
            P(),
            P("row", "col", None, None, None),
            P("row", "col", None, None),
            P("row", "col"),
        ),
        out_specs=(P(("col", "row"), None), P(), P()),
        check_vma=False,
    )
```
